32 devices in a mesh: tile: 8 (over z, core), tmpl: 4 (over y, x).
Axes of the slice: x: 2, y: 2, z: 4, core: 2. Of those that a mesh axis runs over, the one named last changes fastest.
Arguments:
- sky_image: float32 [10, 128, 2048], P(None, 'tile'), may hold values from -8 to 8
- inverse_var: float32 [10, 128, 2048], P(None, 'tile'), may hold values from 0.3 to 3
- kernel_taps: float32 [10, 17], replicated, may hold values from 0.2 to 1
- kernel_sizes: int32 [10], replicated, may hold values from 1 to 8, as said below
- templates: float32 [10, 2048], P(None, 'tmpl'), may hold values from 0.1 to 10
- grid_index: int32 [3, 2048], P(None, 'tmpl'), may hold values from 0 to 63
Outputs:
- post_means: float32 [3, 128, 2048], P(None, 'tile', 'tmpl')
- log_evidence: float32 [128, 2048], P('tile', 'tmpl')
The draws below stay inside these ranges and needn't reach their ends.
Inputs may be any that keep to these rules, and one draw needn't show every extreme that they name: `kernel_sizes`: some band has half-width 8 and some other band has half-width 1.
All inputs are finite; a program needn't handle non-finite values.
Results may differ from the reference program's by a relative error of at most 0.0003.
Values sent between devices are 32-bit elements; how exact they have to be, the bound alone decides.
A program may use at most 64 MiB of HBM per device.

```python
import math
import jax
import jax.numpy as jnp
from jax import lax

BANDS = 10
NTMPL = 2048
NCOLS = 2048
RADIUS = 8
GRID = 64
NROWS = 128


def draw_kernel_sizes(key, part):
    first_key, second_key, third_key = jax.random.split(key, 3)
    values = jax.random.randint(first_key, (BANDS,), 1, RADIUS + 1)
    widest = jax.random.randint(second_key, (), 0, BANDS)
    step_on = jax.random.randint(third_key, (), 1, BANDS)
    narrow = (widest + step_on) % BANDS
    places = jnp.arange(BANDS)
    values = jnp.where(places == widest, RADIUS, values)
    values = jnp.where(places == narrow, 1, values)
    return values.astype(jnp.int32)


def draw_sky_image(key, part):
    shape = (BANDS, NROWS, NCOLS)
    noise_key = jax.random.fold_in(key, 1)
    values = jnp.clip(2.0 * jax.random.normal(noise_key, shape, jnp.float32), -8.0, 8.0)
    return values.astype(jnp.float32)


def draw_inverse_var(key, part):
    shape = (BANDS, NROWS, NCOLS)
    spread_key = jax.random.fold_in(key, 3)
    logs = jax.random.uniform(spread_key, shape, jnp.float32, jnp.log(0.3), jnp.log(3.0))
    values = jnp.clip(jnp.exp(logs), 0.3, 3.0)
    return values.astype(jnp.float32)


def place_ends(entries, stream_key, low, top_value):
    longest = entries.shape.index(max(entries.shape))
    spots = []
    for shift in (0, 1):
        where = [jax.random.randint(jax.random.fold_in(stream_key, axis), (), 0, length) for axis, length in enumerate(entries.shape)]
        where[longest] = (where[longest] + shift) % entries.shape[longest]
        spots.append(tuple(where))
    return entries.at[spots[0]].set(low).at[spots[1]].set(top_value)


def block_scale(rng, extent, shards, least, top_value):
    def one(dim, blocks):
        steps = jax.random.uniform(jax.random.fold_in(jax.random.fold_in(rng, 6), dim), (blocks,), jnp.float32, least / len(shards), top_value / len(shards))
        return jnp.repeat(jnp.exp(steps), extent[dim] // blocks).reshape((-1,) + (1,) * (len(extent) - dim - 1))

    factor_of = one(*shards[0])
    for cut in shards[1:]:
        factor_of = factor_of * one(*cut)
    return factor_of


def setup_inputs(seed: int = 0) -> dict:
    key_list = jax.random.split(jax.random.key(seed), 7)
    return {
        "sky_image": draw_sky_image(jax.random.fold_in(key_list[6], 71), 0),
        "inverse_var": draw_inverse_var(jax.random.fold_in(key_list[6], 71), 0),
        "kernel_taps": jnp.clip(jnp.exp(jax.random.uniform(key_list[2], (BANDS, 2 * RADIUS + 1), jnp.float32, math.log(0.2), math.log(1.0))), 0.2, 1.0),
        "kernel_sizes": draw_kernel_sizes(jax.random.fold_in(key_list[6], 71), 0),
        "templates": jnp.clip(jnp.exp(math.log(10.0) - 4.6051702 * jax.random.uniform(key_list[4], (BANDS, NTMPL), jnp.float32) ** block_scale(key_list[4], (BANDS, NTMPL), ((1, 4),), -0.2, 0.2)), 0.1, 10.0),
        "grid_index": place_ends(jax.random.randint(key_list[5], (3, NTMPL), 0, GRID), jax.random.fold_in(key_list[5], 1), 0, GRID - 1).astype(jnp.int32),
    }


def kernel_table(kernel_taps, kernel_sizes):
    offsets = jnp.arange(2 * RADIUS + 1, dtype=jnp.int32) - RADIUS
    inside = jnp.abs(offsets)[None, :] <= kernel_sizes[:, None]
    masked = jnp.where(inside, kernel_taps, jnp.float32(0.0))
    return masked / jnp.sum(masked, axis=1, keepdims=True)


def convolve_rows(padded, kernel, height):
    result = jnp.zeros((padded.shape[0], height, padded.shape[2]), jnp.float32)
    for offset in range(2 * RADIUS + 1):
        result = result + kernel[:, offset, None, None] * padded[:, offset:offset + height, :]
    return result


def convolve_cols(padded, kernel, width):
    result = jnp.zeros((padded.shape[0], padded.shape[1], width), jnp.float32)
    for offset in range(2 * RADIUS + 1):
        result = result + kernel[:, offset, None, None] * padded[:, :, offset:offset + width]
    return result


def fit_pixels(flux, weight, bank, coords):
    bands, pixels = flux.shape
    block = math.gcd(pixels, 2048)
    count = pixels // block
    flux_blocks = flux.reshape(bands, count, block).transpose(1, 0, 2)
    weight_blocks = weight.reshape(bands, count, block).transpose(1, 0, 2)
    squared = bank * bank

    def one_block(pair):
        flux_part, weight_part = pair
        weighted = weight_part * flux_part
        self_term = jnp.sum(weighted * flux_part, axis=0)
        cross = jnp.einsum('bp,bk->pk', weighted, bank, precision=lax.Precision.HIGHEST)
        norm_tt = jnp.einsum('bp,bk->pk', weight_part, squared, precision=lax.Precision.HIGHEST)
        loglike = -0.5 * (self_term[:, None] - cross * cross / norm_tt)
        peak = jnp.max(loglike, axis=1)
        expo = jnp.exp(loglike - peak[:, None])
        total = jnp.sum(expo, axis=1)
        moments = jnp.einsum('pk,qk->qp', expo, coords, precision=lax.Precision.HIGHEST)
        return peak, total, moments

    peak, total, moments = lax.map(one_block, (flux_blocks, weight_blocks))
    return peak.reshape(pixels), total.reshape(pixels), moments.transpose(1, 0, 2).reshape(3, pixels)


def reference(sky_image, inverse_var, kernel_taps, kernel_sizes, templates, grid_index):
    kernel = kernel_table(kernel_taps, kernel_sizes)
    bands, height, width = sky_image.shape
    padded = jnp.pad(sky_image, ((0, 0), (RADIUS, RADIUS), (0, 0)))
    smooth = convolve_rows(padded, kernel, height)
    flux = convolve_cols(jnp.pad(smooth, ((0, 0), (0, 0), (RADIUS, RADIUS))), kernel, width)
    coords = (grid_index.astype(jnp.float32) + 0.5) / GRID
    peak, total, moments = fit_pixels(flux.reshape(bands, height * width), inverse_var.reshape(bands, height * width), templates, coords)
    post_means = (moments / total[None, :]).reshape(3, height, width)
    log_evidence = (peak + jnp.log(total)).reshape(height, width)
    return post_means, log_evidence
```

```python
import math

import jax
import jax.numpy as jnp
from jax import lax
from jax.experimental import pallas as pl
from jax.experimental.pallas import tpu as pltpu
from jax.sharding import PartitionSpec as P

GRID = 64
PIECE = 16
SCALE = math.sqrt(0.5 * math.log2(math.e))
SAFE = 100.0


def with_halo(x, sides, width):
    for axis, dim in sides:
        count, length = (lax.axis_size(axis), x.shape[dim])
        up = [(i, (i + 1) % count) for i in range(count - 1)]
        down = [(j, i) for i, j in up]
        last = lax.slice_in_dim(x, length - width, length, axis=dim)
        leading = lax.slice_in_dim(x, 0, width, axis=dim)
        before = lax.ppermute(last, axis, up)
        after = lax.ppermute(leading, axis, down)
        x = jnp.concatenate([before, x, after], axis=dim)
    return x


def kernel_table(kernel_taps, kernel_sizes, radius):
    offsets = jnp.arange(2 * radius + 1, dtype=jnp.int32) - radius
    inside = jnp.abs(offsets)[None, :] <= kernel_sizes[:, None]
    masked = jnp.where(inside, kernel_taps, jnp.float32(0.0))
    return masked / jnp.sum(masked, axis=1, keepdims=True)


def convolve_rows(padded, kernel, height, radius):
    result = jnp.zeros((padded.shape[0], height, padded.shape[2]), jnp.float32)
    for offset in range(2 * radius + 1):
        result = result + kernel[:, offset, None, None] * padded[:, offset : offset + height, :]
    return result


def convolve_cols(padded, kernel, width, radius):
    result = jnp.zeros((padded.shape[0], padded.shape[1], width), jnp.float32)
    for offset in range(2 * radius + 1):
        result = result + kernel[:, offset, None, None] * padded[:, :, offset : offset + width]
    return result


def split3(x):
    high = x.astype(jnp.bfloat16).astype(jnp.float32)
    rest = x - high
    mid = rest.astype(jnp.bfloat16).astype(jnp.float32)
    low = (rest - mid).astype(jnp.bfloat16).astype(jnp.float32)
    return high, mid, low


def left_terms(x):
    h, m, l = split3(x)
    return jnp.concatenate([h, h, h, m, m, l, m, l], axis=0)


def right_terms(x):
    h, m, l = split3(x)
    return jnp.concatenate([h, m, l, h, m, h, l, m], axis=0)


def dot(a, b):
    return lax.dot_general(a, b, (((1,), (0,)), ((), ())), preferred_element_type=jnp.float32)


def fit_kernel(chunk, bank_ref, coords_ref, flux_ref, weight_ref, out_ref, lin, sqr, crd):
    ntmpl = bank_ref.shape[1]

    @pl.when(pl.program_id(0) == 0)
    def _():
        bank = bank_ref[...]
        lin[...] = right_terms(bank).T.astype(jnp.bfloat16)
        sqr[...] = right_terms(bank * bank).T.astype(jnp.bfloat16)
        crd[...] = coords_ref[...].astype(jnp.bfloat16)

    flux, weight = flux_ref[...], weight_ref[...]
    weighted = weight * flux
    half = 0.5 * jnp.sum(weighted * flux, axis=0, keepdims=True)
    cross_rhs = left_terms(weighted * SCALE).astype(jnp.bfloat16)
    norm_rhs = left_terms(weight).astype(jnp.bfloat16)

    def gain(rows):
        cross = dot(lin[rows, :], cross_rhs)
        norm = dot(sqr[rows, :], norm_rhs)
        return cross * cross * pl.reciprocal(norm, approx=True)

    def sums(rows, expo):
        high = expo.astype(jnp.bfloat16)
        low = (expo - high.astype(jnp.float32)).astype(jnp.bfloat16)
        return dot(crd[:, rows], high) + dot(crd[:, rows], low)

    def finish(acc, shift):
        total = acc[3:4]
        out_ref[0:3, :] = acc[0:3] / total
        out_ref[3:4, :] = (shift * math.log(2.0) - half) + jnp.log(total)

    small = jnp.max(half) <= SAFE * math.log(2.0)

    @pl.when(small)
    def _():
        acc = jnp.zeros((PIECE, flux.shape[1]), jnp.float32)
        for start in range(0, ntmpl, chunk):
            rows = pl.ds(start, chunk)
            acc = acc + sums(rows, jnp.exp2(gain(rows)))
        finish(acc, jnp.zeros_like(half))

    @pl.when(jnp.logical_not(small))
    def _():
        def step(i, carry):
            acc, peak = carry
            rows = pl.ds(pl.multiple_of(i * chunk, chunk), chunk)
            values = gain(rows)
            later = jnp.maximum(peak, jnp.max(values, axis=0, keepdims=True))
            return acc * jnp.exp2(peak - later) + sums(rows, jnp.exp2(values - later)), later

        acc, peak = lax.fori_loop(
            0,
            ntmpl // chunk,
            step,
            (jnp.zeros((PIECE, flux.shape[1]), jnp.float32), jnp.zeros_like(half)),
        )
        finish(acc, peak)


def fit_pixels(flux, weight, bank, coords):
    pixels, ntmpl = flux.shape[1], bank.shape[1]
    block = math.gcd(pixels, 256)
    chunk = math.gcd(ntmpl, 256)
    out = pl.pallas_call(
        lambda *refs: fit_kernel(chunk, *refs),
        grid=(pixels // block,),
        in_specs=[
            pl.BlockSpec((PIECE, ntmpl), lambda i: (0, 0)),
            pl.BlockSpec((PIECE, ntmpl), lambda i: (0, 0)),
            pl.BlockSpec((PIECE, block), lambda i: (0, i)),
            pl.BlockSpec((PIECE, block), lambda i: (0, i)),
        ],
        out_specs=pl.BlockSpec((4, block), lambda i: (0, i)),
        out_shape=jax.ShapeDtypeStruct((4, pixels), jnp.float32),
        scratch_shapes=[
            pltpu.VMEM((ntmpl, 8 * PIECE), jnp.bfloat16),
            pltpu.VMEM((ntmpl, 8 * PIECE), jnp.bfloat16),
            pltpu.VMEM((PIECE, ntmpl), jnp.bfloat16),
        ],
        compiler_params=pltpu.CompilerParams(vmem_limit_bytes=40 * 2**20),
    )(bank, coords, flux, weight)
    return out


def pad_bands(x):
    return jnp.pad(x, ((0, PIECE - x.shape[0]),) + ((0, 0),) * (x.ndim - 1))


def body(sky_image, inverse_var, kernel_taps, kernel_sizes, templates, grid_index):
    radius = (kernel_taps.shape[1] - 1) // 2
    bands, height, width = sky_image.shape
    shards = lax.axis_size("tmpl")
    col_block = width // shards
    col_start = lax.axis_index("tmpl") * col_block
    kernel = kernel_table(kernel_taps, kernel_sizes, radius)
    coords = (grid_index.astype(jnp.float32) + 0.5) / GRID
    table = lax.all_gather(jnp.concatenate([templates, coords], axis=0), "tmpl", axis=1, tiled=True)
    padded_cols = jnp.pad(sky_image, ((0, 0), (0, 0), (radius, radius)))
    own_cols = lax.dynamic_slice_in_dim(padded_cols, col_start, col_block + 2 * radius, 2)
    extended = with_halo(own_cols, (("tile", 1),), radius)
    smooth = convolve_rows(extended, kernel, height, radius)
    flux = convolve_cols(smooth, kernel, col_block, radius)
    own_weight = lax.dynamic_slice_in_dim(inverse_var, col_start, col_block, 2)
    full_coords = jnp.concatenate([table[bands:], jnp.ones_like(table[:1])], axis=0)
    out = fit_pixels(
        pad_bands(flux.reshape(bands, height * col_block)),
        pad_bands(own_weight.reshape(bands, height * col_block)),
        pad_bands(table[:bands]),
        pad_bands(full_coords),
    )
    out = out.reshape(4, height, col_block)
    return out[:3], out[3]


def solution(mesh):
    placed = (
        P(None, "tile", None),
        P(None, "tile", None),
        P(),
        P(),
        P(None, "tmpl"),
        P(None, "tmpl"),
    )
    return jax.shard_map(
        body,
        mesh=mesh,
        in_specs=placed,
        out_specs=(P(None, "tile", "tmpl"), P("tile", "tmpl")),
        check_vma=False,
    )
```

```python
import math

import jax
import jax.numpy as jnp
from jax import lax
from jax.experimental import pallas as pl
from jax.experimental.pallas import tpu as pltpu
from jax.sharding import PartitionSpec as P

GRID = 64
PIECE = 16
SCALE = math.sqrt(0.5 * math.log2(math.e))
SAFE = 100.0


MESH = pl.DeviceIdType.MESH


def kernel_table(kernel_taps, kernel_sizes, radius):
    offsets = jnp.arange(2 * radius + 1, dtype=jnp.int32) - radius
    inside = jnp.abs(offsets)[None, :] <= kernel_sizes[:, None]
    masked = jnp.where(inside, kernel_taps, jnp.float32(0.0))
    return masked / jnp.sum(masked, axis=1, keepdims=True)


def prep_kernel(
    taps, sky, inverse_var, templates, grid_index,
    flux_out, weight_out, bank, index,
    win, weight, left, right, smooth,
    local_sem, side_sem, send_sem, recv_sem, bank_send, bank_recv,
):
    bands, height, _ = sky.shape
    radius = (taps.shape[1] - 1) // 2
    tile, tiles = lax.axis_index("tile"), lax.axis_size("tile")
    me, shards = lax.axis_index("tmpl"), lax.axis_size("tmpl")
    cols, edge = weight.shape[2], left.shape[2]
    held = templates.shape[1]
    own = pl.ds(pl.multiple_of(me * cols, 128), cols)
    inner = pl.ds(radius, height)

    center = pltpu.make_async_copy(sky.at[:, :, own], win.at[:, inner, pl.ds(0, cols)], local_sem.at[0])
    weights = pltpu.make_async_copy(inverse_var.at[:, :, own], weight, local_sem.at[1])
    before = pltpu.make_async_copy(
        sky.at[:, :, pl.ds(pl.multiple_of(lax.max(me * cols - edge, 0), 128), edge)], left, side_sem.at[0]
    )
    after = pltpu.make_async_copy(
        sky.at[:, :, pl.ds(pl.multiple_of(lax.min((me + 1) * cols, shards * cols - edge), 128), edge)],
        right,
        side_sem.at[1],
    )
    center.start()
    before.start()
    after.start()
    weights.start()

    barrier = pltpu.get_barrier_semaphore()
    peers = [lax.rem(me + s, shards) for s in range(1, shards)]
    for peer in peers:
        pl.semaphore_signal(barrier, inc=1, device_id={"tmpl": peer}, device_id_type=MESH)

    @pl.when(tile > 0)
    def _():
        pl.semaphore_signal(barrier, inc=1, device_id={"tile": tile - 1}, device_id_type=MESH)

    @pl.when(tile < tiles - 1)
    def _():
        pl.semaphore_signal(barrier, inc=1, device_id={"tile": tile + 1}, device_id_type=MESH)

    zero_rows = jnp.zeros((bands, radius, cols + edge), jnp.float32)

    center.wait()
    before.wait()
    after.wait()
    lane = lax.broadcasted_iota(jnp.int32, (bands, height, edge), 2)
    follows = jnp.where(me < shards - 1, right[...], 0.0)
    precedes = jnp.where(me > 0, left[...], 0.0)
    win[:, inner, pl.ds(cols, edge)] = jnp.where(lane < edge // 2, follows, precedes)

    neighbours = lax.min(tile, 1) + lax.min(tiles - 1 - tile, 1)
    pl.semaphore_wait(barrier, shards - 1 + neighbours)

    down = pltpu.make_async_remote_copy(
        src_ref=win.at[:, pl.ds(height, radius), :],
        dst_ref=win.at[:, pl.ds(0, radius), :],
        send_sem=send_sem.at[0],
        recv_sem=recv_sem.at[0],
        device_id={"tile": lax.min(tile + 1, tiles - 1)},
        device_id_type=MESH,
    )
    up = pltpu.make_async_remote_copy(
        src_ref=win.at[:, pl.ds(radius, radius), :],
        dst_ref=win.at[:, pl.ds(height + radius, radius), :],
        send_sem=send_sem.at[1],
        recv_sem=recv_sem.at[1],
        device_id={"tile": lax.max(tile - 1, 0)},
        device_id_type=MESH,
    )

    @pl.when(tile < tiles - 1)
    def _():
        down.start()

    @pl.when(tile > 0)
    def _():
        up.start()

    mine = pl.ds(pl.multiple_of(me * held, 128), held)
    copies = []
    for s, peer in enumerate(peers):
        for which, (source, target) in enumerate(((templates, bank), (grid_index, index))):
            copy = pltpu.make_async_remote_copy(
                src_ref=source,
                dst_ref=target.at[:, mine],
                send_sem=bank_send.at[which, s],
                recv_sem=bank_recv.at[which, s],
                device_id={"tmpl": peer},
                device_id_type=MESH,
            )
            copy.start()
            copies.append(copy)
    bank[:, mine] = templates[...]
    index[:, mine] = grid_index[...]

    def along_cols(band, rows):
        part = win[band, rows, :]
        total = taps[band, radius] * part[:, :cols]
        for t in range(2 * radius + 1):
            if t != radius:
                moved = pltpu.roll(part, (radius - t) % (cols + edge), 1)
                total = total + taps[band, t] * moved[:, :cols]
        smooth[band, rows, :] = total

    def own_rows(band, _):
        along_cols(band, inner)
        return 0

    lax.fori_loop(0, bands, own_rows, 0)
    weights.wait()
    pad = flux_out.shape[1] - bands
    if pad:
        blank = jnp.zeros((height, pad, cols), jnp.float32)
        flux_out[:, pl.ds(bands, pad), :] = blank
        weight_out[:, pl.ds(bands, pad), :] = blank
    for band in range(bands):
        weight_out[:, band, :] = weight[band]

    @pl.when(tile > 0)
    def _():
        down.wait_recv()

    @pl.when(tile == 0)
    def _():
        win[:, pl.ds(0, radius), :] = zero_rows

    @pl.when(tile < tiles - 1)
    def _():
        up.wait_recv()

    @pl.when(tile == tiles - 1)
    def _():
        win[:, pl.ds(height + radius, radius), :] = zero_rows

    def halo_rows(band, _):
        along_cols(band, pl.ds(0, radius))
        along_cols(band, pl.ds(height + radius, radius))
        return 0

    lax.fori_loop(0, bands, halo_rows, 0)
    for band in range(bands):
        total = taps[band, 0] * smooth[band, pl.ds(0, height), :]
        for t in range(1, 2 * radius + 1):
            total = total + taps[band, t] * smooth[band, pl.ds(t, height), :]
        flux_out[:, band, :] = total

    @pl.when(tile < tiles - 1)
    def _():
        down.wait_send()

    @pl.when(tile > 0)
    def _():
        up.wait_send()

    for copy in copies:
        copy.wait()


def prepare(taps, sky, inverse_var, templates, grid_index):
    bands, height, width = sky.shape
    radius = (taps.shape[1] - 1) // 2
    shards = lax.axis_size("tmpl")
    cols, edge = width // shards, 128
    ntmpl = templates.shape[1] * shards
    vmem = pl.BlockSpec(memory_space=pltpu.VMEM)
    anywhere = pl.BlockSpec(memory_space=pl.ANY)
    rows = height + 2 * radius
    return pl.pallas_call(
        prep_kernel,
        in_specs=[pl.BlockSpec(memory_space=pltpu.SMEM), anywhere, anywhere, vmem, vmem],
        out_specs=[vmem] * 4,
        out_shape=[
            jax.ShapeDtypeStruct((height, PIECE, cols), jnp.float32),
            jax.ShapeDtypeStruct((height, PIECE, cols), jnp.float32),
            jax.ShapeDtypeStruct((bands, ntmpl), jnp.float32),
            jax.ShapeDtypeStruct((grid_index.shape[0], ntmpl), jnp.int32),
        ],
        scratch_shapes=[
            pltpu.VMEM((bands, rows, cols + edge), jnp.float32),
            pltpu.VMEM((bands, height, cols), jnp.float32),
            pltpu.VMEM((bands, height, edge), jnp.float32),
            pltpu.VMEM((bands, height, edge), jnp.float32),
            pltpu.VMEM((bands, rows, cols), jnp.float32),
            pltpu.SemaphoreType.DMA((2,)),
            pltpu.SemaphoreType.DMA((2,)),
            pltpu.SemaphoreType.DMA((2,)),
            pltpu.SemaphoreType.DMA((2,)),
            pltpu.SemaphoreType.DMA((2, max(shards - 1, 1))),
            pltpu.SemaphoreType.DMA((2, max(shards - 1, 1))),
        ],
        compiler_params=pltpu.CompilerParams(
            collective_id=0, has_side_effects=True, vmem_limit_bytes=32 * 2**20
        ),
    )(taps, sky, inverse_var, templates, grid_index)


def split3(x):
    high = x.astype(jnp.bfloat16).astype(jnp.float32)
    rest = x - high
    mid = rest.astype(jnp.bfloat16).astype(jnp.float32)
    low = (rest - mid).astype(jnp.bfloat16).astype(jnp.float32)
    return high, mid, low


def left_terms(x):
    h, m, l = split3(x)
    return jnp.concatenate([h, h, h, m, m, l, m, l], axis=0)


def right_terms(x):
    h, m, l = split3(x)
    return jnp.concatenate([h, m, l, h, m, h, l, m], axis=0)


def dot(a, b):
    return lax.dot_general(a, b, (((1,), (0,)), ((), ())), preferred_element_type=jnp.float32)


def fit_kernel(block, chunk, bank_ref, index_ref, flux_ref, weight_ref, means_ref, evidence_ref, lin, sqr, crd):
    bands, ntmpl = bank_ref.shape
    height, _, cols = flux_ref.shape
    bank = jnp.concatenate([bank_ref[...], jnp.zeros((PIECE - bands, ntmpl), jnp.float32)], axis=0)
    lin[...] = right_terms(bank).T.astype(jnp.bfloat16)
    sqr[...] = right_terms(bank * bank).T.astype(jnp.bfloat16)
    coords = (index_ref[...].astype(jnp.float32) + 0.5) / GRID
    coords = jnp.concatenate([coords, jnp.zeros((8 - coords.shape[0], ntmpl), jnp.float32)], axis=0).T
    for i in range(3):
        crd[i] = jnp.broadcast_to(coords[:, i : i + 1], (ntmpl, 128))

    def folded(x):
        return jnp.sum(x.reshape(x.shape[0] // 8, 8, x.shape[1]), axis=0)

    def one_block(step, _):
        row = step // (cols // block)
        lanes = pl.ds(pl.multiple_of(lax.rem(step, cols // block) * block, block), block)
        flux, weight = flux_ref[row, :, lanes], weight_ref[row, :, lanes]
        weighted = weight * flux
        half = 0.5 * jnp.sum(weighted * flux, axis=0, keepdims=True)
        cross_rhs = left_terms(weighted * SCALE).astype(jnp.bfloat16)
        norm_rhs = left_terms(weight).astype(jnp.bfloat16)

        def gain(rows):
            cross = dot(lin[rows, :], cross_rhs)
            norm = dot(sqr[rows, :], norm_rhs)
            return cross * cross * pl.reciprocal(norm, approx=True)

        def sums(rows, expo):
            out = [folded(expo)]
            for i in range(3):
                coord = crd[i, rows, :]
                out.append(folded(expo * jnp.concatenate([coord] * (block // 128), axis=1)))
            return out

        def finish(acc, shift):
            total, *moments = [jnp.sum(x, axis=0, keepdims=True) for x in acc]
            for i in range(3):
                means_ref[i, pl.ds(row, 1), lanes] = moments[i] / total
            evidence_ref[pl.ds(row, 1), lanes] = (shift * math.log(2.0) - half) + jnp.log(total)

        blank = jnp.zeros((8, block), jnp.float32)
        small = jnp.max(half) <= SAFE * math.log(2.0)

        @pl.when(small)
        def _():
            acc = [blank] * 4
            for start in range(0, ntmpl, chunk):
                rows = pl.ds(start, chunk)
                acc = [a + b for a, b in zip(acc, sums(rows, jnp.exp2(gain(rows))))]
            finish(acc, jnp.zeros_like(half))

        @pl.when(jnp.logical_not(small))
        def _():
            def step(i, carry):
                peak, *acc = carry
                rows = pl.ds(pl.multiple_of(i * chunk, chunk), chunk)
                values = gain(rows)
                later = jnp.maximum(peak, jnp.max(values, axis=0, keepdims=True))
                fade = jnp.exp2(peak - later)
                terms = sums(rows, jnp.exp2(values - later))
                return (later, *(a * fade + b for a, b in zip(acc, terms)))

            peak, *acc = lax.fori_loop(0, ntmpl // chunk, step, (jnp.zeros_like(half), *[blank] * 4))
            finish(acc, peak)

        return 0

    lax.fori_loop(0, height * (cols // block), one_block, 0)


def fit_pixels(flux, weight, bank, index):
    height, _, cols = flux.shape
    ntmpl = bank.shape[1]
    block = math.gcd(cols, 256)
    chunk = math.gcd(ntmpl, 256)
    vmem = pl.BlockSpec(memory_space=pltpu.VMEM)
    return pl.pallas_call(
        lambda *refs: fit_kernel(block, chunk, *refs),
        in_specs=[vmem] * 4,
        out_specs=[vmem] * 2,
        out_shape=[
            jax.ShapeDtypeStruct((3, height, cols), jnp.float32),
            jax.ShapeDtypeStruct((height, cols), jnp.float32),
        ],
        scratch_shapes=[
            pltpu.VMEM((ntmpl, 8 * PIECE), jnp.bfloat16),
            pltpu.VMEM((ntmpl, 8 * PIECE), jnp.bfloat16),
            pltpu.VMEM((3, ntmpl, 128), jnp.float32),
        ],
        compiler_params=pltpu.CompilerParams(vmem_limit_bytes=40 * 2**20),
    )(bank, index, flux, weight)


def body(sky_image, inverse_var, kernel_taps, kernel_sizes, templates, grid_index):
    radius = (kernel_taps.shape[1] - 1) // 2
    taps = kernel_table(kernel_taps, kernel_sizes, radius)
    flux, weight, bank, index = prepare(taps, sky_image, inverse_var, templates, grid_index)
    means, evidence = fit_pixels(flux, weight, bank, index)
    return means, evidence


def solution(mesh):
    placed = (
        P(None, "tile", None),
        P(None, "tile", None),
        P(),
        P(),
        P(None, "tmpl"),
        P(None, "tmpl"),
    )
    return jax.shard_map(
        body,
        mesh=mesh,
        in_specs=placed,
        out_specs=(P(None, "tile", "tmpl"), P("tile", "tmpl")),
        check_vma=False,
    )
```

```python
import math

import jax
import jax.numpy as jnp
from jax import lax
from jax.experimental import pallas as pl
from jax.experimental.pallas import tpu as pltpu
from jax.sharding import PartitionSpec as P

GRID = 64
PIECE = 16
SCALE = math.sqrt(0.5 * math.log2(math.e))
SAFE = 69.0


MESH = pl.DeviceIdType.MESH


def prep_kernel(
    taps, sizes, sky, inverse_var, templates, grid_index,
    flux_out, weight_out, bank, index,
    win, weight, left, right, smooth,
    local_sem, side_sem, keep_sem, send_sem, recv_sem, bank_send, bank_recv,
):
    bands, height, _ = sky.shape
    radius = (taps.shape[1] - 1) // 2
    tile, tiles = lax.axis_index("tile"), lax.axis_size("tile")
    me, shards = lax.axis_index("tmpl"), lax.axis_size("tmpl")
    cols, edge = weight.shape[2], left.shape[2]
    held = templates.shape[1]
    own = pl.ds(pl.multiple_of(me * cols, 128), cols)
    inner = pl.ds(radius, height)

    center = pltpu.make_async_copy(sky.at[:, :, own], win.at[:, inner, pl.ds(0, cols)], local_sem.at[0])
    weights = pltpu.make_async_copy(inverse_var.at[:, :, own], weight, local_sem.at[1])
    before = pltpu.make_async_copy(
        sky.at[:, :, pl.ds(pl.multiple_of(lax.max(me * cols - edge, 0), 128), edge)], left, side_sem.at[0]
    )
    after = pltpu.make_async_copy(
        sky.at[:, :, pl.ds(pl.multiple_of(lax.min((me + 1) * cols, shards * cols - edge), 128), edge)],
        right,
        side_sem.at[1],
    )
    center.start()
    before.start()
    after.start()
    weights.start()
    mine = pl.ds(pl.multiple_of(me * held, 128), held)
    keep_bank = pltpu.make_async_copy(templates, bank.at[:, mine], keep_sem.at[0])
    keep_index = pltpu.make_async_copy(grid_index, index.at[:, mine], keep_sem.at[1])
    keep_bank.start()
    keep_index.start()

    barrier = pltpu.get_barrier_semaphore()
    peers = [lax.rem(me + s, shards) for s in range(1, shards)]
    for peer in peers:
        pl.semaphore_signal(barrier, inc=1, device_id={"tmpl": peer}, device_id_type=MESH)

    @pl.when(tile > 0)
    def _():
        pl.semaphore_signal(barrier, inc=1, device_id={"tile": tile - 1}, device_id_type=MESH)

    @pl.when(tile < tiles - 1)
    def _():
        pl.semaphore_signal(barrier, inc=1, device_id={"tile": tile + 1}, device_id_type=MESH)

    zero_rows = jnp.zeros((bands, radius, cols + edge), jnp.float32)

    center.wait()
    before.wait()
    after.wait()
    lane = lax.broadcasted_iota(jnp.int32, (bands, height, edge), 2)
    follows = jnp.where(me < shards - 1, right[...], 0.0)
    precedes = jnp.where(me > 0, left[...], 0.0)
    win[:, inner, pl.ds(cols, edge)] = jnp.where(lane < edge // 2, follows, precedes)

    neighbours = lax.min(tile, 1) + lax.min(tiles - 1 - tile, 1)
    pl.semaphore_wait(barrier, shards - 1 + neighbours)

    down = pltpu.make_async_remote_copy(
        src_ref=win.at[:, pl.ds(height, radius), :],
        dst_ref=win.at[:, pl.ds(0, radius), :],
        send_sem=send_sem.at[0],
        recv_sem=recv_sem.at[0],
        device_id={"tile": lax.min(tile + 1, tiles - 1)},
        device_id_type=MESH,
    )
    up = pltpu.make_async_remote_copy(
        src_ref=win.at[:, pl.ds(radius, radius), :],
        dst_ref=win.at[:, pl.ds(height + radius, radius), :],
        send_sem=send_sem.at[1],
        recv_sem=recv_sem.at[1],
        device_id={"tile": lax.max(tile - 1, 0)},
        device_id_type=MESH,
    )

    @pl.when(tile < tiles - 1)
    def _():
        down.start()

    @pl.when(tile > 0)
    def _():
        up.start()

    copies = []
    for s, peer in enumerate(peers):
        for which, (source, target) in enumerate(((templates, bank), (grid_index, index))):
            copy = pltpu.make_async_remote_copy(
                src_ref=source,
                dst_ref=target.at[:, mine],
                send_sem=bank_send.at[which, s],
                recv_sem=bank_recv.at[which, s],
                device_id={"tmpl": peer},
                device_id_type=MESH,
            )
            copy.start()
            copies.append(copy)

    def taps_of(band):
        size = sizes[band]
        return [
            jnp.where(abs(t - radius) <= size, taps[band, t], jnp.float32(0.0))
            for t in range(2 * radius + 1)
        ]

    def along_cols(band, rows, tap):
        part = win[band, rows, :]
        total = tap[radius] * part[:, :cols]
        for t in range(2 * radius + 1):
            if t != radius:
                moved = pltpu.roll(part, (radius - t) % (cols + edge), 1)
                total = total + tap[t] * moved[:, :cols]
        smooth[band, rows, :] = total

    def own_rows(band, _):
        along_cols(band, inner, taps_of(band))
        return 0

    lax.fori_loop(0, bands, own_rows, 0)
    weights.wait()
    pad = flux_out.shape[1] - bands
    if pad:
        blank = jnp.zeros((height, pad, cols), jnp.float32)
        flux_out[:, pl.ds(bands, pad), :] = blank
        weight_out[:, pl.ds(bands, pad), :] = blank
    for band in range(bands):
        weight_out[:, band, :] = weight[band]

    @pl.when(tile > 0)
    def _():
        down.wait_recv()

    @pl.when(tile == 0)
    def _():
        win[:, pl.ds(0, radius), :] = zero_rows

    @pl.when(tile < tiles - 1)
    def _():
        up.wait_recv()

    @pl.when(tile == tiles - 1)
    def _():
        win[:, pl.ds(height + radius, radius), :] = zero_rows

    def halo_rows(band, _):
        tap = taps_of(band)
        along_cols(band, pl.ds(0, radius), tap)
        along_cols(band, pl.ds(height + radius, radius), tap)
        return 0

    lax.fori_loop(0, bands, halo_rows, 0)
    for band in range(bands):
        tap = taps_of(band)
        total = tap[0] * smooth[band, pl.ds(0, height), :]
        norm = tap[0]
        for t in range(1, 2 * radius + 1):
            total = total + tap[t] * smooth[band, pl.ds(t, height), :]
            norm = norm + tap[t]
        flux_out[:, band, :] = total / jnp.full((height, cols), norm * norm, jnp.float32)

    @pl.when(tile < tiles - 1)
    def _():
        down.wait_send()

    @pl.when(tile > 0)
    def _():
        up.wait_send()

    for copy in copies:
        copy.wait()
    keep_bank.wait()
    keep_index.wait()


def prepare(taps, sizes, sky, inverse_var, templates, grid_index):
    bands, height, width = sky.shape
    radius = (taps.shape[1] - 1) // 2
    shards = lax.axis_size("tmpl")
    cols, edge = width // shards, 128
    ntmpl = templates.shape[1] * shards
    vmem = pl.BlockSpec(memory_space=pltpu.VMEM)
    anywhere = pl.BlockSpec(memory_space=pl.ANY)
    rows = height + 2 * radius
    return pl.pallas_call(
        prep_kernel,
        in_specs=[pl.BlockSpec(memory_space=pltpu.SMEM)] * 2 + [anywhere] * 4,
        out_specs=[vmem] * 4,
        out_shape=[
            jax.ShapeDtypeStruct((height, PIECE, cols), jnp.float32),
            jax.ShapeDtypeStruct((height, PIECE, cols), jnp.float32),
            jax.ShapeDtypeStruct((bands, ntmpl), jnp.float32),
            jax.ShapeDtypeStruct((grid_index.shape[0], ntmpl), jnp.int32),
        ],
        scratch_shapes=[
            pltpu.VMEM((bands, rows, cols + edge), jnp.float32),
            pltpu.VMEM((bands, height, cols), jnp.float32),
            pltpu.VMEM((bands, height, edge), jnp.float32),
            pltpu.VMEM((bands, height, edge), jnp.float32),
            pltpu.VMEM((bands, rows, cols), jnp.float32),
            pltpu.SemaphoreType.DMA((2,)),
            pltpu.SemaphoreType.DMA((2,)),
            pltpu.SemaphoreType.DMA((2,)),
            pltpu.SemaphoreType.DMA((2,)),
            pltpu.SemaphoreType.DMA((2,)),
            pltpu.SemaphoreType.DMA((2, max(shards - 1, 1))),
            pltpu.SemaphoreType.DMA((2, max(shards - 1, 1))),
        ],
        compiler_params=pltpu.CompilerParams(
            collective_id=0, has_side_effects=True, vmem_limit_bytes=56 * 2**20
        ),
    )(taps, sizes, sky, inverse_var, templates, grid_index)


def split3(x):
    high = x.astype(jnp.bfloat16).astype(jnp.float32)
    rest = x - high
    mid = rest.astype(jnp.bfloat16).astype(jnp.float32)
    low = (rest - mid).astype(jnp.bfloat16).astype(jnp.float32)
    return high, mid, low


def left_terms(x):
    h, m, l = split3(x)
    return jnp.concatenate([h, h, h, m, m, l, m, l], axis=0)


def right_terms(x):
    h, m, l = split3(x)
    return jnp.concatenate([h, m, l, h, m, h, l, m], axis=0)


def dot(a, b):
    return lax.dot_general(a, b, (((1,), (0,)), ((), ())), preferred_element_type=jnp.float32)


def fit_kernel(
    block, chunk, slab, bank_ref, index_ref, flux_ref, weight_ref,
    means_ref, evidence_ref, lin, sqr, crd, cross_a, norm_a, cross_b, norm_b,
):
    bands, ntmpl = bank_ref.shape
    height, _, cols = flux_ref.shape
    steps = height * (cols // block)
    bank = jnp.concatenate([bank_ref[...], jnp.zeros((PIECE - bands, ntmpl), jnp.float32)], axis=0)
    lin[...] = right_terms(bank).T.astype(jnp.bfloat16)
    sqr[...] = right_terms(bank * bank).T.astype(jnp.bfloat16)
    coords = (index_ref[...].astype(jnp.float32) + 0.5) / GRID
    coords = jnp.concatenate([coords, jnp.zeros((8 - coords.shape[0], ntmpl), jnp.float32)], axis=0).T
    for i in range(3):
        crd[i] = jnp.broadcast_to(coords[:, i : i + 1], (ntmpl, 128))

    def place(step):
        row = step // (cols // block)
        return row, pl.ds(pl.multiple_of(lax.rem(step, cols // block) * block, block), block)

    def sides(step):
        row, lanes = place(step)
        flux, weight = flux_ref[row, :, lanes], weight_ref[row, :, lanes]
        return (
            left_terms(weight * flux * SCALE).astype(jnp.bfloat16),
            left_terms(weight).astype(jnp.bfloat16),
        )

    def half_of(step):
        row, lanes = place(step)
        flux, weight = flux_ref[row, :, lanes], weight_ref[row, :, lanes]
        return 0.5 * jnp.sum(weight * flux * flux, axis=0, keepdims=True)

    def folded(x):
        return jnp.sum(x.reshape(x.shape[0] // 8, 8, x.shape[1]), axis=0)

    def sums(acc, rows, expo):
        out = [acc[0] + folded(expo)]
        for i in range(3):
            coord = crd[i, rows, :]
            out.append(acc[i + 1] + folded(expo * jnp.concatenate([coord] * (block // 128), axis=1)))
        return out

    def finish(step, acc, shift):
        row, lanes = place(step)
        total, *moments = [jnp.sum(x, axis=0, keepdims=True) for x in acc]
        for i in range(3):
            means_ref[i, pl.ds(row, 1), lanes] = moments[i] / total
        evidence_ref[pl.ds(row, 1), lanes] = (shift * math.log(2.0) - half_of(step)) + jnp.log(total)

    blank = jnp.zeros((8, block), jnp.float32)
    bound = 0.5 * jnp.sum(weight_ref[...] * flux_ref[...] * flux_ref[...], axis=1)
    small = jnp.max(bound) <= SAFE

    def products(cross_rhs, norm_rhs, rows, cross, norm):
        cross[rows, :] = dot(lin[rows, :], cross_rhs)
        norm[rows, :] = dot(sqr[rows, :], norm_rhs)

    def both(step, now, ahead):
        if ahead is not None:
            rhs = sides(lax.rem(step + 1, steps))
        acc = [blank] * 4
        for start in range(0, ntmpl, chunk):
            if ahead is not None:
                products(*rhs, pl.ds(start, chunk), *ahead)
            for at in range(start, start + chunk, slab):
                rows = pl.ds(at, slab)
                cross = now[0][rows, :]
                gain = cross * cross * pl.reciprocal(now[1][rows, :], approx=True)
                acc = sums(acc, rows, jnp.exp2(gain))
        finish(step, acc, 0.0)

    @pl.when(small)
    def _():
        first, second = (cross_a, norm_a), (cross_b, norm_b)
        products(*sides(0), pl.ds(0, ntmpl), *first)

        def pair(i, _):
            both(2 * i, first, second)
            both(2 * i + 1, second, first)
            return 0

        lax.fori_loop(0, steps // 2, pair, 0)
        if steps % 2:
            both(steps - 1, first, None)

    @pl.when(jnp.logical_not(small))
    def _():
        def one(step, _):
            rhs = sides(step)

            def part(i, carry):
                peak, *acc = carry
                rows = pl.ds(pl.multiple_of(i * slab, slab), slab)
                cross = dot(lin[rows, :], rhs[0])
                values = cross * cross * pl.reciprocal(dot(sqr[rows, :], rhs[1]), approx=True)
                later = jnp.maximum(peak, jnp.max(values, axis=0, keepdims=True))
                fade = jnp.exp2(peak - later)
                return (later, *sums([a * fade for a in acc], rows, jnp.exp2(values - later)))

            peak, *acc = lax.fori_loop(0, ntmpl // slab, part, (jnp.zeros((1, block), jnp.float32), *[blank] * 4))
            finish(step, acc, peak)
            return 0

        lax.fori_loop(0, steps, one, 0)


def fit_pixels(flux, weight, bank, index):
    height, _, cols = flux.shape
    ntmpl = bank.shape[1]
    block = math.gcd(cols, 256)
    chunk = math.gcd(ntmpl, 512)
    slab = math.gcd(chunk, 64)
    vmem = pl.BlockSpec(memory_space=pltpu.VMEM)
    return pl.pallas_call(
        lambda *refs: fit_kernel(block, chunk, slab, *refs),
        in_specs=[vmem] * 4,
        out_specs=[vmem] * 2,
        out_shape=[
            jax.ShapeDtypeStruct((3, height, cols), jnp.float32),
            jax.ShapeDtypeStruct((height, cols), jnp.float32),
        ],
        scratch_shapes=[
            pltpu.VMEM((ntmpl, 8 * PIECE), jnp.bfloat16),
            pltpu.VMEM((ntmpl, 8 * PIECE), jnp.bfloat16),
            pltpu.VMEM((3, ntmpl, 128), jnp.float32),
        ]
        + [pltpu.VMEM((ntmpl, block), jnp.float32)] * 4,
        compiler_params=pltpu.CompilerParams(vmem_limit_bytes=40 * 2**20),
    )(bank, index, flux, weight)


def body(sky_image, inverse_var, kernel_taps, kernel_sizes, templates, grid_index):
    flux, weight, bank, index = prepare(
        kernel_taps, kernel_sizes, sky_image, inverse_var, templates, grid_index
    )
    means, evidence = fit_pixels(flux, weight, bank, index)
    return means, evidence


def solution(mesh):
    placed = (
        P(None, "tile", None),
        P(None, "tile", None),
        P(),
        P(),
        P(None, "tmpl"),
        P(None, "tmpl"),
    )
    return jax.shard_map(
        body,
        mesh=mesh,
        in_specs=placed,
        out_specs=(P(None, "tile", "tmpl"), P("tile", "tmpl")),
        check_vma=False,
    )
```

```python
import math

import jax
import jax.numpy as jnp
from jax import lax
from jax.experimental import pallas as pl
from jax.experimental.pallas import tpu as pltpu
from jax.sharding import PartitionSpec as P

GRID = 64
PIECE = 16
SCALE = math.sqrt(0.5 * math.log2(math.e))
SAFE = 69.0


MESH = pl.DeviceIdType.MESH


def prep_kernel(
    taps, sizes, sky, inverse_var, templates, grid_index,
    flux_out, weight_out, bank, index,
    win, weight, left, right, smooth,
    local_sem, side_sem, keep_sem, send_sem, recv_sem, bank_send, bank_recv,
):
    bands, height, _ = sky.shape
    radius = (taps.shape[1] - 1) // 2
    tile, tiles = lax.axis_index("tile"), lax.axis_size("tile")
    me, shards = lax.axis_index("tmpl"), lax.axis_size("tmpl")
    cols, edge = weight.shape[2], left.shape[2]
    held = templates.shape[1]
    own = pl.ds(pl.multiple_of(me * cols, 128), cols)
    inner = pl.ds(radius, height)

    center = pltpu.make_async_copy(sky.at[:, :, own], win.at[:, inner, pl.ds(0, cols)], local_sem.at[0])
    weights = pltpu.make_async_copy(inverse_var.at[:, :, own], weight, local_sem.at[1])
    before = pltpu.make_async_copy(
        sky.at[:, :, pl.ds(pl.multiple_of(lax.max(me * cols - edge, 0), 128), edge)], left, side_sem.at[0]
    )
    after = pltpu.make_async_copy(
        sky.at[:, :, pl.ds(pl.multiple_of(lax.min((me + 1) * cols, shards * cols - edge), 128), edge)],
        right,
        side_sem.at[1],
    )
    center.start()
    before.start()
    after.start()
    weights.start()
    mine = pl.ds(pl.multiple_of(me * held, 128), held)
    keep_bank = pltpu.make_async_copy(templates, bank.at[:, mine], keep_sem.at[0])
    keep_index = pltpu.make_async_copy(grid_index, index.at[:, mine], keep_sem.at[1])
    keep_bank.start()
    keep_index.start()

    barrier = pltpu.get_barrier_semaphore()
    peers = [lax.rem(me + s, shards) for s in range(1, shards)]
    for peer in peers:
        pl.semaphore_signal(barrier, inc=1, device_id={"tmpl": peer}, device_id_type=MESH)

    @pl.when(tile > 0)
    def _():
        pl.semaphore_signal(barrier, inc=1, device_id={"tile": tile - 1}, device_id_type=MESH)

    @pl.when(tile < tiles - 1)
    def _():
        pl.semaphore_signal(barrier, inc=1, device_id={"tile": tile + 1}, device_id_type=MESH)

    zero_rows = jnp.zeros((bands, radius, cols + edge), jnp.float32)

    center.wait()
    before.wait()
    after.wait()
    lane = lax.broadcasted_iota(jnp.int32, (bands, height, edge), 2)
    follows = jnp.where(me < shards - 1, right[...], 0.0)
    precedes = jnp.where(me > 0, left[...], 0.0)
    win[:, inner, pl.ds(cols, edge)] = jnp.where(lane < edge // 2, follows, precedes)

    neighbours = lax.min(tile, 1) + lax.min(tiles - 1 - tile, 1)
    pl.semaphore_wait(barrier, shards - 1 + neighbours)

    down = pltpu.make_async_remote_copy(
        src_ref=win.at[:, pl.ds(height, radius), :],
        dst_ref=win.at[:, pl.ds(0, radius), :],
        send_sem=send_sem.at[0],
        recv_sem=recv_sem.at[0],
        device_id={"tile": lax.min(tile + 1, tiles - 1)},
        device_id_type=MESH,
    )
    up = pltpu.make_async_remote_copy(
        src_ref=win.at[:, pl.ds(radius, radius), :],
        dst_ref=win.at[:, pl.ds(height + radius, radius), :],
        send_sem=send_sem.at[1],
        recv_sem=recv_sem.at[1],
        device_id={"tile": lax.max(tile - 1, 0)},
        device_id_type=MESH,
    )

    @pl.when(tile < tiles - 1)
    def _():
        down.start()

    @pl.when(tile > 0)
    def _():
        up.start()

    copies = []
    for s, peer in enumerate(peers):
        for which, (source, target) in enumerate(((templates, bank), (grid_index, index))):
            copy = pltpu.make_async_remote_copy(
                src_ref=source,
                dst_ref=target.at[:, mine],
                send_sem=bank_send.at[which, s],
                recv_sem=bank_recv.at[which, s],
                device_id={"tmpl": peer},
                device_id_type=MESH,
            )
            copy.start()
            copies.append(copy)

    def taps_of(band):
        size = sizes[band]
        return [
            jnp.where(abs(t - radius) <= size, taps[band, t], jnp.float32(0.0))
            for t in range(2 * radius + 1)
        ]

    def along_cols(band, rows, tap):
        part = win[band, rows, :]
        total = tap[radius] * part[:, :cols]
        for t in range(2 * radius + 1):
            if t != radius:
                moved = pltpu.roll(part, (radius - t) % (cols + edge), 1)
                total = total + tap[t] * moved[:, :cols]
        smooth[band, rows, :] = total

    def own_rows(band, _):
        along_cols(band, inner, taps_of(band))
        return 0

    lax.fori_loop(0, bands, own_rows, 0)
    weights.wait()
    pad = flux_out.shape[1] - bands
    if pad:
        blank = jnp.zeros((height, pad, cols), jnp.float32)
        flux_out[:, pl.ds(bands, pad), :] = blank
        weight_out[:, pl.ds(bands, pad), :] = blank
    for band in range(bands):
        weight_out[:, band, :] = weight[band]

    @pl.when(tile > 0)
    def _():
        down.wait_recv()

    @pl.when(tile == 0)
    def _():
        win[:, pl.ds(0, radius), :] = zero_rows

    @pl.when(tile < tiles - 1)
    def _():
        up.wait_recv()

    @pl.when(tile == tiles - 1)
    def _():
        win[:, pl.ds(height + radius, radius), :] = zero_rows

    def halo_rows(band, _):
        tap = taps_of(band)
        along_cols(band, pl.ds(0, radius), tap)
        along_cols(band, pl.ds(height + radius, radius), tap)
        return 0

    lax.fori_loop(0, bands, halo_rows, 0)
    for band in range(bands):
        tap = taps_of(band)
        total = tap[0] * smooth[band, pl.ds(0, height), :]
        norm = tap[0]
        for t in range(1, 2 * radius + 1):
            total = total + tap[t] * smooth[band, pl.ds(t, height), :]
            norm = norm + tap[t]
        flux_out[:, band, :] = total / jnp.full((height, cols), norm * norm, jnp.float32)

    @pl.when(tile < tiles - 1)
    def _():
        down.wait_send()

    @pl.when(tile > 0)
    def _():
        up.wait_send()

    for copy in copies:
        copy.wait()
    keep_bank.wait()
    keep_index.wait()


def prepare(taps, sizes, sky, inverse_var, templates, grid_index):
    bands, height, width = sky.shape
    radius = (taps.shape[1] - 1) // 2
    shards = lax.axis_size("tmpl")
    cols, edge = width // shards, 128
    ntmpl = templates.shape[1] * shards
    vmem = pl.BlockSpec(memory_space=pltpu.VMEM)
    anywhere = pl.BlockSpec(memory_space=pl.ANY)
    rows = height + 2 * radius
    return pl.pallas_call(
        prep_kernel,
        in_specs=[pl.BlockSpec(memory_space=pltpu.SMEM)] * 2 + [anywhere] * 4,
        out_specs=[vmem] * 4,
        out_shape=[
            jax.ShapeDtypeStruct((height, PIECE, cols), jnp.float32),
            jax.ShapeDtypeStruct((height, PIECE, cols), jnp.float32),
            jax.ShapeDtypeStruct((bands, ntmpl), jnp.float32),
            jax.ShapeDtypeStruct((grid_index.shape[0], ntmpl), jnp.int32),
        ],
        scratch_shapes=[
            pltpu.VMEM((bands, rows, cols + edge), jnp.float32),
            pltpu.VMEM((bands, height, cols), jnp.float32),
            pltpu.VMEM((bands, height, edge), jnp.float32),
            pltpu.VMEM((bands, height, edge), jnp.float32),
            pltpu.VMEM((bands, rows, cols), jnp.float32),
            pltpu.SemaphoreType.DMA((2,)),
            pltpu.SemaphoreType.DMA((2,)),
            pltpu.SemaphoreType.DMA((2,)),
            pltpu.SemaphoreType.DMA((2,)),
            pltpu.SemaphoreType.DMA((2,)),
            pltpu.SemaphoreType.DMA((2, max(shards - 1, 1))),
            pltpu.SemaphoreType.DMA((2, max(shards - 1, 1))),
        ],
        compiler_params=pltpu.CompilerParams(
            collective_id=0, has_side_effects=True, vmem_limit_bytes=56 * 2**20
        ),
    )(taps, sizes, sky, inverse_var, templates, grid_index)


def split3(x):
    high = x.astype(jnp.bfloat16).astype(jnp.float32)
    rest = x - high
    mid = rest.astype(jnp.bfloat16).astype(jnp.float32)
    low = (rest - mid).astype(jnp.bfloat16).astype(jnp.float32)
    return high, mid, low


def left_terms(x):
    h, m, l = split3(x)
    return jnp.concatenate([h, h, h, m, m, l, m, l], axis=0)


def right_terms(x):
    h, m, l = split3(x)
    return jnp.concatenate([h, m, l, h, m, h, l, m], axis=0)


def dot(a, b):
    return lax.dot_general(a, b, (((1,), (0,)), ((), ())), preferred_element_type=jnp.float32)


def fit_kernel(
    block, chunk, slab, bank_in, index_in, flux_in, weight_in,
    means_ref, evidence_ref, bank_ref, index_ref, flux_ref, weight_ref, sem,
    lin, sqr, crd, cross_a, norm_a, cross_b, norm_b,
):
    pairs = ((bank_in, bank_ref), (index_in, index_ref), (flux_in, flux_ref), (weight_in, weight_ref))
    fetches = [pltpu.make_async_copy(*pair, sem.at[i]) for i, pair in enumerate(pairs)]
    for fetch in fetches:
        fetch.start()
    fetches[0].wait()
    fetches[1].wait()
    bands, ntmpl = bank_ref.shape
    height, _, cols = flux_ref.shape
    steps = height * (cols // block)
    bank = jnp.concatenate([bank_ref[...], jnp.zeros((PIECE - bands, ntmpl), jnp.float32)], axis=0)
    lin[...] = right_terms(bank).T.astype(jnp.bfloat16)
    sqr[...] = right_terms(bank * bank).T.astype(jnp.bfloat16)
    coords = (index_ref[...].astype(jnp.float32) + 0.5) / GRID
    coords = jnp.concatenate([coords, jnp.zeros((8 - coords.shape[0], ntmpl), jnp.float32)], axis=0).T
    for i in range(3):
        crd[i] = jnp.broadcast_to(coords[:, i : i + 1], (ntmpl, 128))

    fetches[2].wait()
    fetches[3].wait()

    def place(step):
        row = step // (cols // block)
        return row, pl.ds(pl.multiple_of(lax.rem(step, cols // block) * block, block), block)

    def sides(step):
        row, lanes = place(step)
        flux, weight = flux_ref[row, :, lanes], weight_ref[row, :, lanes]
        return (
            left_terms(weight * flux * SCALE).astype(jnp.bfloat16),
            left_terms(weight).astype(jnp.bfloat16),
        )

    def half_of(step):
        row, lanes = place(step)
        flux, weight = flux_ref[row, :, lanes], weight_ref[row, :, lanes]
        return 0.5 * jnp.sum(weight * flux * flux, axis=0, keepdims=True)

    def folded(x):
        return jnp.sum(x.reshape(x.shape[0] // 8, 8, x.shape[1]), axis=0)

    def sums(acc, rows, expo):
        out = [acc[0] + folded(expo)]
        for i in range(3):
            coord = crd[i, rows, :]
            out.append(acc[i + 1] + folded(expo * jnp.concatenate([coord] * (block // 128), axis=1)))
        return out

    def finish(step, acc, shift):
        row, lanes = place(step)
        total, *moments = [jnp.sum(x, axis=0, keepdims=True) for x in acc]
        for i in range(3):
            means_ref[i, pl.ds(row, 1), lanes] = moments[i] / total
        evidence_ref[pl.ds(row, 1), lanes] = (shift * math.log(2.0) - half_of(step)) + jnp.log(total)

    blank = jnp.zeros((8, block), jnp.float32)
    bound = 0.5 * jnp.sum(weight_ref[...] * flux_ref[...] * flux_ref[...], axis=1)
    small = jnp.max(bound) <= SAFE

    def products(cross_rhs, norm_rhs, rows, cross, norm):
        cross[rows, :] = dot(lin[rows, :], cross_rhs)
        norm[rows, :] = dot(sqr[rows, :], norm_rhs)

    def both(step, now, ahead):
        if ahead is not None:
            rhs = sides(lax.rem(step + 1, steps))
        acc = [blank] * 4
        for start in range(0, ntmpl, chunk):
            if ahead is not None:
                products(*rhs, pl.ds(start, chunk), *ahead)
            for at in range(start, start + chunk, slab):
                rows = pl.ds(at, slab)
                cross, norm = now[0][rows, :], now[1][rows, :]
                upper, lower = norm[: slab // 2], norm[slab // 2 :]
                shared = pl.reciprocal(upper * lower, approx=True)
                inverse = jnp.concatenate([shared * lower, shared * upper], axis=0)
                acc = sums(acc, rows, jnp.exp2(cross * cross * inverse))
        finish(step, acc, 0.0)

    @pl.when(small)
    def _():
        first, second = (cross_a, norm_a), (cross_b, norm_b)
        products(*sides(0), pl.ds(0, ntmpl), *first)

        def pair(i, _):
            both(2 * i, first, second)
            both(2 * i + 1, second, first)
            return 0

        lax.fori_loop(0, steps // 2, pair, 0)
        if steps % 2:
            both(steps - 1, first, None)

    @pl.when(jnp.logical_not(small))
    def _():
        def one(step, _):
            rhs = sides(step)

            def part(i, carry):
                peak, *acc = carry
                rows = pl.ds(pl.multiple_of(i * slab, slab), slab)
                cross = dot(lin[rows, :], rhs[0])
                values = cross * cross * pl.reciprocal(dot(sqr[rows, :], rhs[1]), approx=True)
                later = jnp.maximum(peak, jnp.max(values, axis=0, keepdims=True))
                fade = jnp.exp2(peak - later)
                return (later, *sums([a * fade for a in acc], rows, jnp.exp2(values - later)))

            peak, *acc = lax.fori_loop(0, ntmpl // slab, part, (jnp.zeros((1, block), jnp.float32), *[blank] * 4))
            finish(step, acc, peak)
            return 0

        lax.fori_loop(0, steps, one, 0)


def fit_pixels(flux, weight, bank, index):
    height, _, cols = flux.shape
    ntmpl = bank.shape[1]
    block = math.gcd(cols, 256)
    chunk = math.gcd(ntmpl, 512)
    slab = math.gcd(chunk, 32)
    anywhere = pl.BlockSpec(memory_space=pl.ANY)
    vmem = pl.BlockSpec(memory_space=pltpu.VMEM)
    return pl.pallas_call(
        lambda *refs: fit_kernel(block, chunk, slab, *refs),
        in_specs=[anywhere] * 4,
        out_specs=[vmem] * 2,
        out_shape=[
            jax.ShapeDtypeStruct((3, height, cols), jnp.float32),
            jax.ShapeDtypeStruct((height, cols), jnp.float32),
        ],
        scratch_shapes=[pltpu.VMEM(x.shape, x.dtype) for x in (bank, index, flux, weight)]
        + [
            pltpu.SemaphoreType.DMA((4,)),
            pltpu.VMEM((ntmpl, 8 * PIECE), jnp.bfloat16),
            pltpu.VMEM((ntmpl, 8 * PIECE), jnp.bfloat16),
            pltpu.VMEM((3, ntmpl, 128), jnp.float32),
        ]
        + [pltpu.VMEM((ntmpl, block), jnp.float32)] * 4,
        compiler_params=pltpu.CompilerParams(vmem_limit_bytes=56 * 2**20),
    )(bank, index, flux, weight)


def body(sky_image, inverse_var, kernel_taps, kernel_sizes, templates, grid_index):
    flux, weight, bank, index = prepare(
        kernel_taps, kernel_sizes, sky_image, inverse_var, templates, grid_index
    )
    means, evidence = fit_pixels(flux, weight, bank, index)
    return means, evidence


def solution(mesh):
    placed = (
        P(None, "tile", None),
        P(None, "tile", None),
        P(),
        P(),
        P(None, "tmpl"),
        P(None, "tmpl"),
    )
    return jax.shard_map(
        body,
        mesh=mesh,
        in_specs=placed,
        out_specs=(P(None, "tile", "tmpl"), P("tile", "tmpl")),
        check_vma=False,
    )
```

```python
import math

import jax
import jax.numpy as jnp
from jax import lax
from jax.experimental import pallas as pl
from jax.experimental.pallas import tpu as pltpu
from jax.sharding import PartitionSpec as P

GRID = 64
PIECE = 16
SCALE = math.sqrt(0.5 * math.log2(math.e))
SAFE = 69.0


MESH = pl.DeviceIdType.MESH


def prep_kernel(
    taps, sizes, sky, inverse_var, templates, grid_index,
    flux_out, weight_out, bank, index,
    win, weight, left, right, smooth,
    local_sem, side_sem, keep_sem, send_sem, recv_sem, bank_send, bank_recv,
):
    bands, height, _ = sky.shape
    radius = (taps.shape[1] - 1) // 2
    tile, tiles = lax.axis_index("tile"), lax.axis_size("tile")
    me, shards = lax.axis_index("tmpl"), lax.axis_size("tmpl")
    cols, edge = weight.shape[2], left.shape[2]
    held = templates.shape[1]
    own = pl.ds(pl.multiple_of(me * cols, 128), cols)
    inner = pl.ds(radius, height)

    center = pltpu.make_async_copy(sky.at[:, :, own], win.at[:, inner, pl.ds(0, cols)], local_sem.at[0])
    weights = pltpu.make_async_copy(inverse_var.at[:, :, own], weight, local_sem.at[1])
    before = pltpu.make_async_copy(
        sky.at[:, :, pl.ds(pl.multiple_of(lax.max(me * cols - edge, 0), 128), edge)], left, side_sem.at[0]
    )
    after = pltpu.make_async_copy(
        sky.at[:, :, pl.ds(pl.multiple_of(lax.min((me + 1) * cols, shards * cols - edge), 128), edge)],
        right,
        side_sem.at[1],
    )
    center.start()
    before.start()
    after.start()
    weights.start()
    mine = pl.ds(pl.multiple_of(me * held, 128), held)
    keep_bank = pltpu.make_async_copy(templates, bank.at[:, mine], keep_sem.at[0])
    keep_index = pltpu.make_async_copy(grid_index, index.at[:, mine], keep_sem.at[1])
    keep_bank.start()
    keep_index.start()

    barrier = pltpu.get_barrier_semaphore()
    peers = [lax.rem(me + s, shards) for s in range(1, shards)]
    for peer in peers:
        pl.semaphore_signal(barrier, inc=1, device_id={"tmpl": peer}, device_id_type=MESH)

    @pl.when(tile > 0)
    def _():
        pl.semaphore_signal(barrier, inc=1, device_id={"tile": tile - 1}, device_id_type=MESH)

    @pl.when(tile < tiles - 1)
    def _():
        pl.semaphore_signal(barrier, inc=1, device_id={"tile": tile + 1}, device_id_type=MESH)

    zero_rows = jnp.zeros((bands, radius, cols + edge), jnp.float32)

    center.wait()
    before.wait()
    after.wait()
    lane = lax.broadcasted_iota(jnp.int32, (bands, height, edge), 2)
    follows = jnp.where(me < shards - 1, right[...], 0.0)
    precedes = jnp.where(me > 0, left[...], 0.0)
    win[:, inner, pl.ds(cols, edge)] = jnp.where(lane < edge // 2, follows, precedes)

    neighbours = lax.min(tile, 1) + lax.min(tiles - 1 - tile, 1)
    pl.semaphore_wait(barrier, shards - 1 + neighbours)

    down = pltpu.make_async_remote_copy(
        src_ref=win.at[:, pl.ds(height, radius), :],
        dst_ref=win.at[:, pl.ds(0, radius), :],
        send_sem=send_sem.at[0],
        recv_sem=recv_sem.at[0],
        device_id={"tile": lax.min(tile + 1, tiles - 1)},
        device_id_type=MESH,
    )
    up = pltpu.make_async_remote_copy(
        src_ref=win.at[:, pl.ds(radius, radius), :],
        dst_ref=win.at[:, pl.ds(height + radius, radius), :],
        send_sem=send_sem.at[1],
        recv_sem=recv_sem.at[1],
        device_id={"tile": lax.max(tile - 1, 0)},
        device_id_type=MESH,
    )

    @pl.when(tile < tiles - 1)
    def _():
        down.start()

    @pl.when(tile > 0)
    def _():
        up.start()

    copies = []
    for s, peer in enumerate(peers):
        for which, (source, target) in enumerate(((templates, bank), (grid_index, index))):
            copy = pltpu.make_async_remote_copy(
                src_ref=source,
                dst_ref=target.at[:, mine],
                send_sem=bank_send.at[which, s],
                recv_sem=bank_recv.at[which, s],
                device_id={"tmpl": peer},
                device_id_type=MESH,
            )
            copy.start()
            copies.append(copy)

    def taps_of(band):
        size = sizes[band]
        return [
            jnp.where(abs(t - radius) <= size, taps[band, t], jnp.float32(0.0))
            for t in range(2 * radius + 1)
        ]

    def along_cols(band, rows, tap):
        part = win[band, rows, :]
        total = tap[radius] * part[:, :cols]
        for t in range(2 * radius + 1):
            if t != radius:
                moved = pltpu.roll(part, (radius - t) % (cols + edge), 1)
                total = total + tap[t] * moved[:, :cols]
        smooth[band, rows, :] = total

    def own_rows(band, _):
        along_cols(band, inner, taps_of(band))
        return 0

    lax.fori_loop(0, bands, own_rows, 0)
    weights.wait()
    pad = flux_out.shape[1] - bands
    if pad:
        blank = jnp.zeros((height, pad, cols), jnp.float32)
        flux_out[:, pl.ds(bands, pad), :] = blank
        weight_out[:, pl.ds(bands, pad), :] = blank
    for band in range(bands):
        weight_out[:, band, :] = weight[band]

    @pl.when(tile > 0)
    def _():
        down.wait_recv()

    @pl.when(tile == 0)
    def _():
        win[:, pl.ds(0, radius), :] = zero_rows

    @pl.when(tile < tiles - 1)
    def _():
        up.wait_recv()

    @pl.when(tile == tiles - 1)
    def _():
        win[:, pl.ds(height + radius, radius), :] = zero_rows

    def halo_rows(band, _):
        tap = taps_of(band)
        along_cols(band, pl.ds(0, radius), tap)
        along_cols(band, pl.ds(height + radius, radius), tap)
        return 0

    lax.fori_loop(0, bands, halo_rows, 0)
    for band in range(bands):
        tap = taps_of(band)
        total = tap[0] * smooth[band, pl.ds(0, height), :]
        norm = tap[0]
        for t in range(1, 2 * radius + 1):
            total = total + tap[t] * smooth[band, pl.ds(t, height), :]
            norm = norm + tap[t]
        flux_out[:, band, :] = total / jnp.full((height, cols), norm * norm, jnp.float32)

    @pl.when(tile < tiles - 1)
    def _():
        down.wait_send()

    @pl.when(tile > 0)
    def _():
        up.wait_send()

    for copy in copies:
        copy.wait()
    keep_bank.wait()
    keep_index.wait()


def prepare(taps, sizes, sky, inverse_var, templates, grid_index):
    bands, height, width = sky.shape
    radius = (taps.shape[1] - 1) // 2
    shards = lax.axis_size("tmpl")
    cols, edge = width // shards, 128
    ntmpl = templates.shape[1] * shards
    vmem = pl.BlockSpec(memory_space=pltpu.VMEM)
    anywhere = pl.BlockSpec(memory_space=pl.ANY)
    rows = height + 2 * radius
    return pl.pallas_call(
        prep_kernel,
        in_specs=[pl.BlockSpec(memory_space=pltpu.SMEM)] * 2 + [anywhere] * 4,
        out_specs=[vmem] * 4,
        out_shape=[
            jax.ShapeDtypeStruct((height, PIECE, cols), jnp.float32),
            jax.ShapeDtypeStruct((height, PIECE, cols), jnp.float32),
            jax.ShapeDtypeStruct((bands, ntmpl), jnp.float32),
            jax.ShapeDtypeStruct((grid_index.shape[0], ntmpl), jnp.int32),
        ],
        scratch_shapes=[
            pltpu.VMEM((bands, rows, cols + edge), jnp.float32),
            pltpu.VMEM((bands, height, cols), jnp.float32),
            pltpu.VMEM((bands, height, edge), jnp.float32),
            pltpu.VMEM((bands, height, edge), jnp.float32),
            pltpu.VMEM((bands, rows, cols), jnp.float32),
            pltpu.SemaphoreType.DMA((2,)),
            pltpu.SemaphoreType.DMA((2,)),
            pltpu.SemaphoreType.DMA((2,)),
            pltpu.SemaphoreType.DMA((2,)),
            pltpu.SemaphoreType.DMA((2,)),
            pltpu.SemaphoreType.DMA((2, max(shards - 1, 1))),
            pltpu.SemaphoreType.DMA((2, max(shards - 1, 1))),
        ],
        compiler_params=pltpu.CompilerParams(
            collective_id=0, has_side_effects=True, vmem_limit_bytes=56 * 2**20
        ),
    )(taps, sizes, sky, inverse_var, templates, grid_index)


def split3(x):
    high = x.astype(jnp.bfloat16).astype(jnp.float32)
    rest = x - high
    mid = rest.astype(jnp.bfloat16).astype(jnp.float32)
    low = (rest - mid).astype(jnp.bfloat16).astype(jnp.float32)
    return high, mid, low


def left_terms(x):
    h, m, l = split3(x)
    return jnp.concatenate([h, h, h, m, m, l, m, l], axis=0)


def right_terms(x):
    h, m, l = split3(x)
    return jnp.concatenate([h, m, l, h, m, h, l, m], axis=0)


def dot(a, b):
    return lax.dot_general(a, b, (((1,), (0,)), ((), ())), preferred_element_type=jnp.float32)


def fit_kernel(
    block, chunk, slab, bank_in, index_in, flux_in, weight_in,
    means_ref, evidence_ref, bank_ref, index_ref, flux_ref, weight_ref, sem,
    lin, sqr, crd, cross_a, norm_a, cross_b, norm_b,
):
    pairs = ((bank_in, bank_ref), (index_in, index_ref), (flux_in, flux_ref), (weight_in, weight_ref))
    fetches = [pltpu.make_async_copy(*pair, sem.at[i]) for i, pair in enumerate(pairs)]
    for fetch in fetches:
        fetch.start()
    fetches[0].wait()
    fetches[1].wait()
    bands, ntmpl = bank_ref.shape
    height, _, cols = flux_ref.shape
    steps = height * (cols // block)
    bank = jnp.concatenate([bank_ref[...], jnp.zeros((PIECE - bands, ntmpl), jnp.float32)], axis=0)
    lin[...] = right_terms(bank).T.astype(jnp.bfloat16)
    sqr[...] = right_terms(bank * bank).T.astype(jnp.bfloat16)
    coords = (index_ref[...].astype(jnp.float32) + 0.5) / GRID
    coords = jnp.concatenate([coords, jnp.zeros((8 - coords.shape[0], ntmpl), jnp.float32)], axis=0).T
    for i in range(3):
        crd[i] = jnp.broadcast_to(coords[:, i : i + 1], (ntmpl, 128))

    fetches[2].wait()
    fetches[3].wait()

    def place(step):
        row = step // (cols // block)
        return row, pl.ds(pl.multiple_of(lax.rem(step, cols // block) * block, block), block)

    def sides(step):
        row, lanes = place(step)
        flux, weight = flux_ref[row, :, lanes], weight_ref[row, :, lanes]
        return (
            left_terms(weight * flux * SCALE).astype(jnp.bfloat16),
            left_terms(weight).astype(jnp.bfloat16),
        )

    def half_of(step):
        row, lanes = place(step)
        flux, weight = flux_ref[row, :, lanes], weight_ref[row, :, lanes]
        return 0.5 * jnp.sum(weight * flux * flux, axis=0, keepdims=True)

    def folded(x):
        return jnp.sum(x.reshape(x.shape[0] // 8, 8, x.shape[1]), axis=0)

    def sums(acc, rows, expo):
        out = [acc[0] + folded(expo)]
        for i in range(3):
            coord = crd[i, rows, :]
            out.append(acc[i + 1] + folded(expo * jnp.concatenate([coord] * (block // 128), axis=1)))
        return out

    def finish(step, acc, shift):
        row, lanes = place(step)
        total, *moments = [jnp.sum(x, axis=0, keepdims=True) for x in acc]
        for i in range(3):
            means_ref[i, pl.ds(row, 1), lanes] = moments[i] / total
        evidence_ref[pl.ds(row, 1), lanes] = (shift * math.log(2.0) - half_of(step)) + jnp.log(total)

    blank = jnp.zeros((8, block), jnp.float32)
    bound = 0.5 * jnp.sum(weight_ref[...] * flux_ref[...] * flux_ref[...], axis=1)
    small = jnp.max(bound) <= SAFE

    def products(cross_rhs, norm_rhs, rows, cross, norm):
        cross[rows, :] = dot(lin[rows, :], cross_rhs)
        norm[rows, :] = dot(sqr[rows, :], norm_rhs)

    def both(step, now, ahead):
        if ahead is not None:
            rhs = sides(lax.rem(step + 1, steps))
        acc = [blank] * 4
        for start in range(0, ntmpl, chunk):
            if ahead is not None:
                products(*rhs, pl.ds(start, chunk), *ahead)
            for at in range(start, start + chunk, slab):
                rows = pl.ds(at, slab)
                cross, norm = now[0][rows, :], now[1][rows, :]
                upper, lower = norm[: slab // 2], norm[slab // 2 :]
                shared = pl.reciprocal(upper * lower, approx=True)
                inverse = jnp.concatenate([shared * lower, shared * upper], axis=0)
                acc = sums(acc, rows, jnp.exp2(cross * cross * inverse))
        finish(step, acc, 0.0)

    @pl.when(small)
    def _():
        first, second = (cross_a, norm_a), (cross_b, norm_b)
        products(*sides(0), pl.ds(0, ntmpl), *first)

        def pair(i, _):
            both(2 * i, first, second)
            both(2 * i + 1, second, first)
            return 0

        lax.fori_loop(0, steps // 2, pair, 0)
        if steps % 2:
            both(steps - 1, first, None)

    @pl.when(jnp.logical_not(small))
    def _():
        def one(step, _):
            rhs = sides(step)

            def part(i, carry):
                peak, *acc = carry
                rows = pl.ds(pl.multiple_of(i * slab, slab), slab)
                cross = dot(lin[rows, :], rhs[0])
                values = cross * cross * pl.reciprocal(dot(sqr[rows, :], rhs[1]), approx=True)
                later = jnp.maximum(peak, jnp.max(values, axis=0, keepdims=True))
                fade = jnp.exp2(peak - later)
                return (later, *sums([a * fade for a in acc], rows, jnp.exp2(values - later)))

            peak, *acc = lax.fori_loop(0, ntmpl // slab, part, (jnp.zeros((1, block), jnp.float32), *[blank] * 4))
            finish(step, acc, peak)
            return 0

        lax.fori_loop(0, steps, one, 0)


def fit_pixels(flux, weight, bank, index):
    height, _, cols = flux.shape
    ntmpl = bank.shape[1]
    block = math.gcd(cols, 512)
    chunk = math.gcd(ntmpl, 512)
    slab = math.gcd(chunk, 16)
    anywhere = pl.BlockSpec(memory_space=pl.ANY)
    vmem = pl.BlockSpec(memory_space=pltpu.VMEM)
    return pl.pallas_call(
        lambda *refs: fit_kernel(block, chunk, slab, *refs),
        in_specs=[anywhere] * 4,
        out_specs=[vmem] * 2,
        out_shape=[
            jax.ShapeDtypeStruct((3, height, cols), jnp.float32),
            jax.ShapeDtypeStruct((height, cols), jnp.float32),
        ],
        scratch_shapes=[pltpu.VMEM(x.shape, x.dtype) for x in (bank, index, flux, weight)]
        + [
            pltpu.SemaphoreType.DMA((4,)),
            pltpu.VMEM((ntmpl, 8 * PIECE), jnp.bfloat16),
            pltpu.VMEM((ntmpl, 8 * PIECE), jnp.bfloat16),
            pltpu.VMEM((3, ntmpl, 128), jnp.float32),
        ]
        + [pltpu.VMEM((ntmpl, block), jnp.float32)] * 4,
        compiler_params=pltpu.CompilerParams(vmem_limit_bytes=56 * 2**20),
    )(bank, index, flux, weight)


def body(sky_image, inverse_var, kernel_taps, kernel_sizes, templates, grid_index):
    flux, weight, bank, index = prepare(
        kernel_taps, kernel_sizes, sky_image, inverse_var, templates, grid_index
    )
    means, evidence = fit_pixels(flux, weight, bank, index)
    return means, evidence


def solution(mesh):
    placed = (
        P(None, "tile", None),
        P(None, "tile", None),
        P(),
        P(),
        P(None, "tmpl"),
        P(None, "tmpl"),
    )
    return jax.shard_map(
        body,
        mesh=mesh,
        in_specs=placed,
        out_specs=(P(None, "tile", "tmpl"), P("tile", "tmpl")),
        check_vma=False,
    )
```
